256 devices in a mesh: face: 16 (over y, x_hi, core), fsdp: 16 (over z, x_lo).
Axes of the slice: x: 4 (x_hi: 2, x_lo: 2; x = x_hi * 2 + x_lo), y: 4, z: 8, core: 2. Of those that a mesh axis runs over, the one named last changes fastest.
Arguments:
- node_features: bfloat16 [98304, 1024], P(('face', 'fsdp')), may hold values from -120 to 120
- norm_gain: float32 [1024], replicated, may hold values from 0.1 to 1.9
- query_weight: bfloat16 [1024, 1024], P('fsdp'), may hold values from -0.2 to 0.2
- key_weight: bfloat16 [1024, 1024], P('fsdp'), may hold values from -6 to 6
- value_weight: bfloat16 [1024, 1024], P('fsdp'), may hold values from -0.1875 to 0.1875
- out_weight: bfloat16 [1024, 1024], P('fsdp'), may hold values from -3 to 3
- cotangent: bfloat16 [98304, 1024], P(('face', 'fsdp')), may hold values from -24 to 24
- pair_mask: int32 [768, 6], P(('face', 'fsdp')), may hold values from 0 to 1, as said below
- border_ids: int32 [256, 3], P(('face', 'fsdp')), may hold values from 0 to 2
Outputs:
- layer_update: bfloat16 [98304, 1024], P(('face', 'fsdp'))
- node_gradient: bfloat16 [98304, 1024], P(('face', 'fsdp'))
- query_gradient: float32 [1024, 1024], P('fsdp')
- key_gradient: float32 [1024, 1024], P('fsdp')
- value_gradient: float32 [1024, 1024], P('fsdp')
- output_gradient: float32 [1024, 1024], P('fsdp')
The draws below stay inside these ranges and needn't reach their ends.
Inputs may be any that keep to these rules, and one draw needn't show every extreme that they name: `pair_mask`: each query tile lists its own tile (the key slot equal to its index within the device), and query tile b mod 3 lists the border slot 3 + b.
All inputs are finite; a program needn't handle non-finite values.
Results may differ from the reference program's by a relative error of at most 0.03.
The reference program's roundings to bfloat16 on the way count: a program that leaves them out, or rounds other values in their place, can miss the bound.
Values may be sent and summed in bfloat16 or wider, within the bound.
No kernel may reach another device: no remote copies, remote signals or barrier semaphores. Data moves between devices by JAX's collectives and lax.ppermute only.
A program may use at most 128 MiB of HBM per device.

```python
import math
import jax
import jax.numpy as jnp
from jax import lax

D = 1024
HEADS = 16
HEAD_DIM = 64
TILE = 128
TILES_DEV = 3
MATCHINGS = 3
NODES = 98304
N_FACE = 16
N_FSDP = 16


def shared_query(key):
    raw = jax.random.normal(jax.random.fold_in(key, 7), (D, D), jnp.float32)
    return jnp.clip(raw * D ** (-0.5), -0.199, 0.199)


def draw_node_features(key, part):
    key = jax.random.fold_in(key, 11)
    first, second, third = jax.random.split(key, 3)
    row_scale = jnp.exp(jax.random.uniform(second, (NODES, 1), jnp.float32, 0.0, math.log(10.0)))
    col_scale = jnp.exp(jax.random.uniform(third, (1, D), jnp.float32, math.log(0.3), math.log(3.0)))
    base = jax.random.normal(first, (NODES, D), jnp.float32)
    base = jnp.clip(base, -4.0, 4.0)
    return (base * row_scale * col_scale).astype(jnp.bfloat16)


def draw_query_weight(key, part):
    return shared_query(key).astype(jnp.bfloat16)


def draw_key_weight(key, part):
    key = jax.random.fold_in(key, 43)
    second = jax.random.fold_in(key, 1)
    noise = jnp.clip(jax.random.normal(second, (D, D), jnp.float32) * D ** (-0.5), -0.2, 0.2)
    return noise.astype(jnp.bfloat16)


def draw_pair_mask(key, part):
    key = jax.random.fold_in(key, 31)
    first, second = jax.random.split(key)
    device_count = N_FACE * N_FSDP
    slot_count = TILES_DEV + MATCHINGS
    level = jax.random.randint(first, (device_count, 1, 1), 10, 96)
    rolls = jax.random.randint(second, (device_count, TILES_DEV, slot_count), 0, 100)
    tile_index = jnp.arange(TILES_DEV)[:, None]
    slot_index = jnp.arange(slot_count)[None, :]
    forced = (tile_index == slot_index) | (slot_index >= TILES_DEV) & (tile_index == (slot_index - TILES_DEV) % TILES_DEV)
    chosen = jnp.where(forced[None], 1, (rolls < level).astype(jnp.int32))
    return chosen.reshape(device_count * TILES_DEV, slot_count).astype(jnp.int32)


def set_ends(entries, stream_key, smallest, high):
    extent = entries.shape
    spot = [jax.random.randint(jax.random.fold_in(stream_key, axis), (), 0, extent[axis]) for axis in range(len(extent))]
    entries = entries.at[tuple(spot)].set(smallest)
    longest = extent.index(max(extent))
    spot[longest] = (spot[longest] + 1) % extent[longest]
    return entries.at[tuple(spot)].set(high)


def spiked(values, rng, source, target, shards_of, factor):
    def block_of(position):
        return (jnp.arange(values.shape[position]) // (values.shape[position] // shards_of)).reshape((-1,) + (1,) * (values.ndim - 1 - position))

    near = jax.random.permutation(rng, shards_of)[block_of(target)]
    second = (block_of(target) + shards_of // 2) % shards_of
    return jnp.where((block_of(source) == near) | (block_of(source) == second), factor * values, values)


def shard_levels(key, dims, cuts, low, top_value):
    loudness, own = 1.0, jax.random.fold_in(key, 6)
    for axis_at, parts in cuts:
        heights = jnp.exp(jax.random.uniform(jax.random.fold_in(own, axis_at), (parts,), jnp.float32, low / len(cuts), top_value / len(cuts)))
        loudness = loudness * jnp.repeat(heights, dims[axis_at] // parts).reshape([-1 if axis == axis_at else 1 for axis in range(len(dims))])
    return loudness


def scatter_about(key, extent, deviation, bound, shards=(), kind=jnp.bfloat16):
    entries = deviation * jax.random.normal(key, extent, jnp.float32)
    if shards:
        entries = entries * shard_levels(key, extent, shards, -0.22, 0.18)
    return jnp.clip(entries, -bound, bound).astype(kind)


def gaussian_with(stream_key, shape, width, bound, cuts, heavy, kind=jnp.bfloat16):
    result = width * jax.random.normal(stream_key, shape, jnp.float32)
    if cuts:
        result = result * shard_levels(stream_key, shape, cuts, -0.22, 0.18)
    return jnp.clip(spiked(result, jax.random.fold_in(stream_key, 3), *heavy), -bound, bound).astype(kind)


def setup_inputs(seed: int = 0) -> dict:
    seeds = jax.random.split(jax.random.key(seed), 10)
    node_features = draw_node_features(jax.random.fold_in(seeds[9], 71), 0)
    norm_gain = jnp.clip(1.0 + 0.18 * jax.random.normal(seeds[1], (D,), jnp.float32), 0.1, 1.9)
    query_weight = draw_query_weight(jax.random.fold_in(seeds[9], 71), 0)
    key_weight = draw_key_weight(jax.random.fold_in(seeds[9], 71), 0)
    value_weight = scatter_about(seeds[4], (D, D), D ** -0.5, 0.1875, ((0, 16),))
    out_weight = scatter_about(seeds[5], (D, D), (max(D // 256, 1)) ** -0.5, 3.0, ((0, 16),))
    cotangent = gaussian_with(seeds[6], (NODES, D), 1.0, 24.0, ((0, 256),), (0, 1, 256, 6.0))
    pair_mask = draw_pair_mask(jax.random.fold_in(seeds[9], 71), 0)
    border_ids = set_ends(jax.random.randint(seeds[8], (N_FACE * N_FSDP, MATCHINGS), 0, TILES_DEV), jax.random.fold_in(seeds[8], 1), 0, TILES_DEV - 1).astype(jnp.int32)
    return dict(node_features=node_features, norm_gain=norm_gain, query_weight=query_weight, key_weight=key_weight, value_weight=value_weight, out_weight=out_weight, cotangent=cotangent, pair_mask=pair_mask, border_ids=border_ids)


epsilon = 1e-06
group_heads = 4

def tile_live(tile_mask):
    wide = jnp.repeat(jnp.repeat(tile_mask, TILE, axis=0), TILE, axis=1)
    return wide > 0

def attend(queries, key_set, value_set, grad_rows, live):
    row_count = queries.shape[0]
    key_count = key_set.shape[0]
    block_width = group_heads * HEAD_DIM
    factor = HEAD_DIM ** (-0.5)
    mask_all = live[None]

    def head_step(step_index, carry):
        out_acc, query_acc, key_acc, value_acc = carry
        offset = (step_index * block_width).astype(jnp.int32)
        query_part = lax.dynamic_slice_in_dim(queries, offset, block_width, 1).astype(jnp.float32).reshape(row_count, group_heads, HEAD_DIM)
        key_part = lax.dynamic_slice_in_dim(key_set, offset, block_width, 1).astype(jnp.float32).reshape(key_count, group_heads, HEAD_DIM)
        value_part = lax.dynamic_slice_in_dim(value_set, offset, block_width, 1).astype(jnp.float32).reshape(key_count, group_heads, HEAD_DIM)
        grad_part = lax.dynamic_slice_in_dim(grad_rows, offset, block_width, 1).astype(jnp.float32).reshape(row_count, group_heads, HEAD_DIM)
        scores = jnp.einsum('ihd,jhd->hij', query_part, key_part) * factor
        top_score = lax.optimization_barrier(jnp.max(jnp.where(mask_all, scores, -jnp.inf), axis=2, keepdims=True))
        expo_terms = jnp.exp(jnp.where(mask_all, scores - top_score, -jnp.inf))
        weights = expo_terms / lax.optimization_barrier(jnp.sum(expo_terms, axis=2, keepdims=True))
        probs_rounded = lax.optimization_barrier(weights.astype(jnp.bfloat16)).astype(jnp.float32)
        attended = jnp.einsum('hij,jhd->ihd', probs_rounded, value_part)
        grad_probs = jnp.einsum('ihd,jhd->hij', grad_part, value_part)
        inner_sum = lax.optimization_barrier(jnp.sum(weights * grad_probs, axis=2, keepdims=True))
        grad_scores = lax.optimization_barrier((weights * (grad_probs - inner_sum) * factor).astype(jnp.bfloat16)).astype(jnp.float32)
        grad_query = jnp.einsum('hij,jhd->ihd', grad_scores, key_part)
        grad_key = jnp.einsum('hij,ihd->jhd', grad_scores, query_part)
        grad_value = jnp.einsum('hij,ihd->jhd', probs_rounded, grad_part)
        out_acc = lax.dynamic_update_slice_in_dim(out_acc, attended.reshape(row_count, block_width), offset, 1)
        query_acc = lax.dynamic_update_slice_in_dim(query_acc, grad_query.reshape(row_count, block_width), offset, 1)
        key_acc = lax.dynamic_update_slice_in_dim(key_acc, grad_key.reshape(key_count, block_width), offset, 1)
        value_acc = lax.dynamic_update_slice_in_dim(value_acc, grad_value.reshape(key_count, block_width), offset, 1)
        return (out_acc, query_acc, key_acc, value_acc)
    start_state = (jnp.zeros((row_count, D), jnp.float32), jnp.zeros((row_count, D), jnp.float32), jnp.zeros((key_count, D), jnp.float32), jnp.zeros((key_count, D), jnp.float32))
    return lax.fori_loop(0, HEADS // group_heads, head_step, start_state)

def reference(node_features, norm_gain, query_weight, key_weight, value_weight, out_weight, cotangent, pair_mask, border_ids):
    devices = N_FACE * N_FSDP
    row_count = TILES_DEV * TILE
    features = node_features.astype(jnp.float32)
    inverse = lax.rsqrt(lax.optimization_barrier(jnp.mean(features * features, axis=1, keepdims=True)) + epsilon)
    normed = (features * inverse * norm_gain).astype(jnp.bfloat16)
    queries = jnp.dot(normed, query_weight, preferred_element_type=jnp.float32).astype(jnp.bfloat16)
    keys = jnp.dot(normed, key_weight, preferred_element_type=jnp.float32).astype(jnp.bfloat16)
    values = jnp.dot(normed, value_weight, preferred_element_type=jnp.float32).astype(jnp.bfloat16)
    grad_attended = jnp.dot(cotangent, out_weight.T, preferred_element_type=jnp.float32).astype(jnp.bfloat16)
    device_ids = jnp.arange(devices, dtype=jnp.int32)
    powers = jnp.array([2 ** bit_number for bit_number in range(MATCHINGS)], dtype=jnp.int32)
    partners = jnp.bitwise_xor(device_ids[:, None] // N_FSDP, powers[None, :]) * N_FSDP + device_ids[:, None] % N_FSDP

    def one_device(device):
        first = (device * row_count).astype(jnp.int32)
        key_parts = [lax.dynamic_slice_in_dim(keys, first, row_count, 0)]
        value_parts = [lax.dynamic_slice_in_dim(values, first, row_count, 0)]
        for bit_number in range(MATCHINGS):
            partner = partners[device, bit_number]
            start = ((partner * TILES_DEV + border_ids[partner, bit_number]) * TILE).astype(jnp.int32)
            key_parts.append(lax.dynamic_slice_in_dim(keys, start, TILE, 0))
            value_parts.append(lax.dynamic_slice_in_dim(values, start, TILE, 0))
        key_set = jnp.concatenate(key_parts, axis=0)
        value_set = jnp.concatenate(value_parts, axis=0)
        live = tile_live(lax.dynamic_slice_in_dim(pair_mask, (device * TILES_DEV).astype(jnp.int32), TILES_DEV, 0))
        query_rows = lax.dynamic_slice_in_dim(queries, first, row_count, 0)
        grad_rows = lax.dynamic_slice_in_dim(grad_attended, first, row_count, 0)
        attended, grad_query, grad_key, grad_value = attend(query_rows, key_set, value_set, grad_rows, live)
        return (attended.astype(jnp.bfloat16), grad_query.astype(jnp.bfloat16), grad_key[:row_count], grad_value[:row_count], grad_key[row_count:].astype(jnp.bfloat16), grad_value[row_count:].astype(jnp.bfloat16))
    attended, grad_queries, own_keys, own_values, halo_keys, halo_values = lax.map(one_device, device_ids)
    attended = attended.reshape(NODES, D)
    grad_queries = grad_queries.reshape(NODES, D)
    layer_update = jnp.dot(attended, out_weight, preferred_element_type=jnp.float32).astype(jnp.bfloat16)
    slots = jnp.arange(MATCHINGS, dtype=jnp.int32)[None, :]
    selector = (border_ids[:, :, None] == jnp.arange(TILES_DEV, dtype=jnp.int32)[None, None, :]).astype(jnp.float32)
    recv_keys = halo_keys.reshape(devices, MATCHINGS, TILE, D)[partners, slots].astype(jnp.float32)
    recv_values = halo_values.reshape(devices, MATCHINGS, TILE, D)[partners, slots].astype(jnp.float32)
    extra_keys = jnp.einsum('abt,abnd->atnd', selector, recv_keys).reshape(devices, row_count, D)
    extra_values = jnp.einsum('abt,abnd->atnd', selector, recv_values).reshape(devices, row_count, D)
    grad_keys = (own_keys + extra_keys).astype(jnp.bfloat16).reshape(NODES, D)
    grad_values = (own_values + extra_values).astype(jnp.bfloat16).reshape(NODES, D)
    grad_normed = jnp.dot(grad_queries, query_weight.T, preferred_element_type=jnp.float32) + jnp.dot(grad_keys, key_weight.T, preferred_element_type=jnp.float32) + jnp.dot(grad_values, value_weight.T, preferred_element_type=jnp.float32)
    scaled = grad_normed * norm_gain
    inner_mean = lax.optimization_barrier(jnp.mean(scaled * features, axis=1, keepdims=True))
    node_gradient = (inverse * scaled - features * inverse ** 3 * inner_mean).astype(jnp.bfloat16)
    query_gradient = jnp.dot(normed.T, grad_queries, preferred_element_type=jnp.float32)
    key_gradient = jnp.dot(normed.T, grad_keys, preferred_element_type=jnp.float32)
    value_gradient = jnp.dot(normed.T, grad_values, preferred_element_type=jnp.float32)
    output_gradient = jnp.dot(attended.T, cotangent, preferred_element_type=jnp.float32)
    return (layer_update, node_gradient, query_gradient, key_gradient, value_gradient, output_gradient)
```

```python
import functools

import jax
import jax.numpy as jnp
from jax import lax
from jax.experimental import pallas as pl
from jax.experimental.pallas import tpu as pltpu
from jax.sharding import Mesh, PartitionSpec as P


TILE = 128
TILES = 3
ROWS = TILE * TILES
PAIR_ROWS = 2 * ROWS
HEAD = 64
HALF = 512
PIECE = 128
epsilon = 1e-06

FACE = ("y", "xh", "core")
PLANE = ("y", "xh")
FSDP = ("z", "xl")
NODES = FACE + FSDP
SWAP = [(0, 1), (1, 0)]


def contract_rows(left, right):
    return lax.dot_general(
        left, right, (((0,), (0,)), ((), ())), preferred_element_type=jnp.float32
    )


def times_transpose(left, right):
    return lax.dot_general(
        left, right, (((1,), (1,)), ((), ())), preferred_element_type=jnp.float32
    )


def dot(left, right):
    return jnp.dot(left, right, preferred_element_type=jnp.float32)


def swap_core(value):
    return lax.ppermute(value, "core", SWAP)


def ordered(mine, theirs, core, axis):
    size = mine.shape[axis]
    three = jnp.concatenate([theirs, mine, theirs], axis=axis)
    return lax.dynamic_slice_in_dim(three, (1 - core) * size, 2 * size, axis)


def attention_kernel(
    mask_ref, ids_ref, q_ref, k_ref, v_ref, g_ref, k1_ref, v1_ref, k2_ref, v2_ref,
    out_ref, gq_ref, gk_ref, gv_ref, bk_ref, bv_ref, score_ref, grad_ref,
):
    lane = lax.broadcasted_iota(jnp.int32, (1, 2 * HEAD), 1)
    column = lax.broadcasted_iota(jnp.int32, (1, ROWS), 1)
    sides = [(lane < HEAD), (lane >= HEAD)]
    zero = jnp.zeros((), jnp.bfloat16)
    border_k, border_v = [], []
    for block in range(2):
        rows = pl.ds(block * ROWS, ROWS)
        other = pl.ds(
            pl.multiple_of((1 - block) * ROWS + ids_ref[1 - block, 0] * TILE, TILE), TILE
        )
        keys = jnp.concatenate([k_ref[rows, :], k_ref[other, :], k1_ref[block], k2_ref[block]], 0)
        values = jnp.concatenate([v_ref[rows, :], v_ref[other, :], v1_ref[block], v2_ref[block]], 0)
        queries = q_ref[rows, :]
        grads = g_ref[rows, :]
        biases = []
        for slot in range(2 * TILES):
            parts = [mask_ref[block * TILES + t, slot] for t in range(TILES)]
            live = jnp.where(
                column < TILE, parts[0], jnp.where(column < 2 * TILE, parts[1], parts[2])
            )
            biases.append(jnp.where(live > 0, 0.0, -1e30).astype(jnp.float32))
        out = gq = gk = gv = None
        for side in sides:
            q_side = jnp.where(side, queries * jnp.bfloat16(0.125), zero)
            g_side = jnp.where(side, grads, zero)
            k_side = jnp.where(side, keys * jnp.bfloat16(0.125), zero)
            v_side = jnp.where(side, values, zero)
            top = None
            for slot in range(2 * TILES):
                span = slice(slot * TILE, (slot + 1) * TILE)
                score = times_transpose(keys[span], q_side) + biases[slot]
                score_ref[span, :] = score
                peak = jnp.max(score, axis=0, keepdims=True)
                top = peak if top is None else jnp.maximum(top, peak)
            total = inner = None
            for slot in range(2 * TILES):
                span = slice(slot * TILE, (slot + 1) * TILE)
                expo = jnp.exp(score_ref[span, :] - top)
                grad = times_transpose(values[span], g_side)
                score_ref[span, :] = expo
                grad_ref[span, :] = grad
                part = jnp.sum(expo, axis=0, keepdims=True)
                cross = jnp.sum(expo * grad, axis=0, keepdims=True)
                total = part if total is None else total + part
                inner = cross if inner is None else inner + cross
            scale = 1.0 / total
            inner = inner * scale
            probs, slopes = [], []
            for slot in range(2 * TILES):
                span = slice(slot * TILE, (slot + 1) * TILE)
                weight = score_ref[span, :] * scale
                probs.append(weight.astype(jnp.bfloat16))
                slopes.append((weight * (grad_ref[span, :] - inner)).astype(jnp.bfloat16))
            probs = jnp.concatenate(probs, 0)
            slopes = jnp.concatenate(slopes, 0)
            parts = (
                contract_rows(v_side, probs),
                contract_rows(k_side, slopes),
                dot(slopes, q_side),
                dot(probs, g_side),
            )
            if out is None:
                out, gq, gk, gv = parts
            else:
                out, gq, gk, gv = out + parts[0], gq + parts[1], gk + parts[2], gv + parts[3]
        out_ref[rows, :] = out.T.astype(jnp.bfloat16)
        gq_ref[rows, :] = gq.T.astype(jnp.bfloat16)
        gk_ref[rows, :] = gk[:ROWS]
        gv_ref[rows, :] = gv[:ROWS]
        border_k.append(gk[ROWS : ROWS + TILE].astype(jnp.bfloat16))
        border_v.append(gv[ROWS : ROWS + TILE].astype(jnp.bfloat16))
        for slot in range(2):
            span = slice(ROWS + (slot + 1) * TILE, ROWS + (slot + 2) * TILE)
            bk_ref[slot, block] = gk[span].astype(jnp.bfloat16)
            bv_ref[slot, block] = gv[span].astype(jnp.bfloat16)
    for block in range(2):
        other = pl.ds(
            pl.multiple_of((1 - block) * ROWS + ids_ref[1 - block, 0] * TILE, TILE), TILE
        )
        gk_ref[other, :] += border_k[block].astype(jnp.float32)
        gv_ref[other, :] += border_v[block].astype(jnp.float32)


def attention(mask, ids, q, kv, g, border1, border2):
    pair = 2 * HEAD
    steps = HALF // pair

    def flat(shift):
        return pl.BlockSpec((PAIR_ROWS, pair), lambda j: (0, j + shift))

    def tile(shift):
        return pl.BlockSpec((2, TILE, pair), lambda j: (0, 0, j + shift))

    smem = pl.BlockSpec(memory_space=pltpu.SMEM)
    border = pl.BlockSpec((2, 2, TILE, pair), lambda j: (0, 0, 0, j))
    return pl.pallas_call(
        attention_kernel,
        grid=(steps,),
        in_specs=[
            smem, smem, flat(0), flat(0), flat(steps), flat(0),
            tile(0), tile(steps), tile(0), tile(steps),
        ],
        out_specs=[flat(0), flat(0), flat(0), flat(0), border, border],
        out_shape=[
            jax.ShapeDtypeStruct((PAIR_ROWS, HALF), jnp.bfloat16),
            jax.ShapeDtypeStruct((PAIR_ROWS, HALF), jnp.bfloat16),
            jax.ShapeDtypeStruct((PAIR_ROWS, HALF), jnp.float32),
            jax.ShapeDtypeStruct((PAIR_ROWS, HALF), jnp.float32),
            jax.ShapeDtypeStruct((2, 2, TILE, HALF), jnp.bfloat16),
            jax.ShapeDtypeStruct((2, 2, TILE, HALF), jnp.bfloat16),
        ],
        scratch_shapes=[
            pltpu.VMEM((2 * ROWS, ROWS), jnp.float32),
            pltpu.VMEM((2 * ROWS, ROWS), jnp.float32),
        ],
        compiler_params=pltpu.CompilerParams(vmem_limit_bytes=40 * 1024 * 1024),
        cost_estimate=pl.CostEstimate(
            flops=15_000_000_000, bytes_accessed=16_000_000, transcendentals=5_000_000
        ),
        name="attention",
    )(mask, ids, q, kv, kv, g, border1, border1, border2, border2)


def spread(value, axes, count):
    copies = jnp.broadcast_to(value[None], (count,) + value.shape)
    return lax.all_to_all(copies, axes, 0, 0, tiled=True)


def norm(features, gain):
    wide = features.astype(jnp.float32)
    inverse = lax.rsqrt(jnp.mean(wide * wide, axis=1, keepdims=True) + epsilon)
    return wide, inverse, (wide * inverse * gain).astype(jnp.bfloat16)


def reduce_half(term, sums):
    pieces = term.astype(jnp.bfloat16).reshape(1024, 8, PIECE).transpose(1, 0, 2)
    arrived = lax.all_to_all(pieces, PLANE, 0, 0, tiled=True)
    part = jnp.sum(arrived.astype(jnp.float32), axis=0).astype(jnp.bfloat16)
    arrived = lax.all_to_all(part.reshape(16, 64, PIECE), FSDP, 0, 0, tiled=True)
    return jnp.sum(arrived.astype(jnp.float32), axis=0).astype(jnp.bfloat16)


def local(
    node_features, norm_gain, query_weight, key_weight, value_weight, out_weight,
    cotangent, pair_mask, border_ids,
):
    core = lax.axis_index("core")
    plane = lax.axis_index("y") * 2 + lax.axis_index("xh")

    def half_of(value, which):
        return lax.dynamic_slice_in_dim(value, which * HALF, HALF, 1)

    first = jnp.concatenate([half_of(key_weight, core), half_of(value_weight, core)], 1)
    second = jnp.concatenate([half_of(query_weight, core), half_of(out_weight, core)], 1)
    piece = lax.dynamic_slice_in_dim(jnp.stack([first, second]), plane * PIECE, PIECE, 2)
    fetched = spread(piece, FSDP, 16)
    first_piece = fetched[:, 0].reshape(1024, PIECE)
    second_piece = fetched[:, 1].reshape(1024, PIECE)
    key_value = spread(first_piece, PLANE, 8).transpose(1, 0, 2).reshape(1024, 1024)

    features = ordered(node_features, swap_core(node_features), core, 0)
    cotangent_half = ordered(
        half_of(cotangent, core), swap_core(half_of(cotangent, 1 - core)), core, 0
    )
    plan = jnp.concatenate([pair_mask, jnp.broadcast_to(border_ids, (TILES, TILES))], 1)
    plan = ordered(plan, swap_core(plan), core, 0)
    mask = plan[:, : 2 * TILES]
    ids = plan[:: TILES, 2 * TILES :]

    normed = norm(features, norm_gain)[2]
    kv = dot(normed, key_value).astype(jnp.bfloat16)
    arrived = []
    for bit, (axis, route) in ((1, ("xh", SWAP)), (2, ("y", [(0, 1), (1, 0), (2, 3), (3, 2)]))):
        sent = jnp.stack(
            [
                lax.dynamic_slice_in_dim(kv, block * ROWS + ids[block, bit] * TILE, TILE, 0)
                for block in range(2)
            ]
        )
        arrived.append(lax.ppermute(sent, axis, route))

    query_out = spread(second_piece, PLANE, 8).transpose(1, 0, 2).reshape(1024, 1024)
    query_half, out_half = query_out[:, :HALF], query_out[:, HALF:]
    q = dot(normed, query_half).astype(jnp.bfloat16)
    grad_part = times_transpose(cotangent_half, out_half)
    grad_attended = (
        half_of(grad_part, core) + swap_core(half_of(grad_part, 1 - core))
    ).astype(jnp.bfloat16)

    attended, grad_q, own_k, own_v, back_k, back_v = attention(
        mask, ids, q, kv, grad_attended, arrived[0], arrived[1]
    )
    returned = []
    for slot, (axis, route) in enumerate((("xh", SWAP), ("y", [(0, 1), (1, 0), (2, 3), (3, 2)]))):
        returned.append(lax.ppermute(jnp.stack([back_k[slot], back_v[slot]]), axis, route))

    attended_all = ordered(attended, swap_core(attended), core, 1)
    update = dot(attended_all, out_half).astype(jnp.bfloat16)
    update_mine = lax.dynamic_slice_in_dim(update, core * ROWS, ROWS, 0)
    update_theirs = lax.dynamic_slice_in_dim(update, (1 - core) * ROWS, ROWS, 0)
    layer_update = ordered(update_mine, swap_core(update_theirs), core, 1)

    term_second = jnp.concatenate(
        [contract_rows(normed, grad_q), contract_rows(attended_all, cotangent_half)], 1
    )
    sum_second = reduce_half(term_second, None)

    selector = (ids[:, 1:, None] == jnp.arange(TILES, dtype=jnp.int32)).astype(jnp.float32)
    extra = sum(
        selector[:, slot, :, None, None].reshape(1, 2, TILES, 1, 1)
        * returned[slot].astype(jnp.float32)[:, :, None]
        for slot in range(2)
    ).reshape(2, PAIR_ROWS, HALF)
    grad_k = (own_k + extra[0]).astype(jnp.bfloat16)
    grad_v = (own_v + extra[1]).astype(jnp.bfloat16)
    grad_kv = jnp.concatenate([grad_k, grad_v], 1)
    sum_first = reduce_half(contract_rows(normed, grad_kv), None)

    grad_normed = times_transpose(grad_q, query_half) + times_transpose(grad_kv, key_value)
    grad_mine = lax.dynamic_slice_in_dim(grad_normed, core * ROWS, ROWS, 0)
    grad_theirs = lax.dynamic_slice_in_dim(grad_normed, (1 - core) * ROWS, ROWS, 0)
    scaled = (grad_mine + swap_core(grad_theirs)) * norm_gain
    wide, inverse, _ = norm(node_features, norm_gain)
    inner_mean = jnp.mean(scaled * wide, axis=1, keepdims=True)
    node_gradient = (inverse * scaled - wide * inverse**3 * inner_mean).astype(jnp.bfloat16)

    gathered = spread(jnp.stack([sum_first, sum_second]), FACE, 16)
    gathered = gathered.reshape(2, 4, 2, 2, 64, PIECE)
    gathered = gathered.transpose(3, 0, 4, 2, 1, 5).reshape(2, 2, 64, 1024).astype(jnp.float32)
    return (
        layer_update, node_gradient, gathered[1, 0], gathered[0, 0], gathered[0, 1], gathered[1, 1]
    )


def solution(mesh):
    fine = Mesh(mesh.devices.reshape(4, 2, 2, 8, 2), NODES)
    rows = P(NODES, None)
    weight = P(FSDP, None)
    return jax.shard_map(
        local,
        mesh=fine,
        in_specs=(rows, P(), weight, weight, weight, weight, rows, rows, rows),
        out_specs=(rows, rows, weight, weight, weight, weight),
        check_vma=False,
    )
```

```python
import functools

import jax
import jax.numpy as jnp
from jax import lax
from jax.experimental import pallas as pl
from jax.experimental.pallas import tpu as pltpu
from jax.sharding import Mesh, PartitionSpec as P


TILE = 128
TILES = 3
ROWS = TILE * TILES
PAIR_ROWS = 2 * ROWS
ALL_ROWS = PAIR_ROWS + 4 * TILE
HEAD = 64
HALF = 512
PART = 256
SLAB = 16
epsilon = 1e-06

FACE = ("y", "xh", "core")
PLANE = ("xl", "y", "xh")
FSDP = ("z", "xl")
NODES = FACE + FSDP
SWAP = [(0, 1), (1, 0)]


def contract_rows(left, right):
    return lax.dot_general(
        left, right, (((0,), (0,)), ((), ())), preferred_element_type=jnp.float32
    )


def times_transpose(left, right):
    return lax.dot_general(
        left, right, (((1,), (1,)), ((), ())), preferred_element_type=jnp.float32
    )


def dot(left, right):
    return jnp.dot(left, right, preferred_element_type=jnp.float32)


def swap_core(value):
    return lax.ppermute(value, "core", SWAP)


def attention_kernel(
    mask_ref, ids_ref, q_ref, k_ref, v_ref, g_ref, *refs
):
    out_ref, gq_ref, own_ref, all_ref, back1_ref, back2_ref, score_ref, grad_ref = refs[-8:]
    lane = lax.broadcasted_iota(jnp.int32, (1, 2 * HEAD), 1)
    column = lax.broadcasted_iota(jnp.int32, (1, ROWS), 1)
    sides = [(lane < HEAD), (lane >= HEAD)]
    zero = jnp.zeros((), jnp.bfloat16)
    step = pl.program_id(0) * 2 * HEAD
    k_span = pl.ds(pl.multiple_of(step, 2 * HEAD), 2 * HEAD)
    v_span = pl.ds(pl.multiple_of(PART + step, 2 * HEAD), 2 * HEAD)
    border_k, border_v = [], []
    for block in range(2):
        rows = pl.ds(block * ROWS, ROWS)
        other = pl.ds(
            pl.multiple_of((1 - block) * ROWS + ids_ref[1 - block, 0] * TILE, TILE), TILE
        )
        far = slice(PAIR_ROWS + block * 2 * TILE, PAIR_ROWS + (block + 1) * 2 * TILE)
        keys = jnp.concatenate([k_ref[rows, :], k_ref[other, :], k_ref[far, :]], 0)
        values = jnp.concatenate([v_ref[rows, :], v_ref[other, :], v_ref[far, :]], 0)
        queries = q_ref[rows, :]
        grads = g_ref[rows, :]
        biases = []
        for slot in range(2 * TILES):
            parts = [mask_ref[block * TILES + t, slot] for t in range(TILES)]
            live = jnp.where(
                column < TILE, parts[0], jnp.where(column < 2 * TILE, parts[1], parts[2])
            )
            biases.append(jnp.where(live > 0, 0.0, -1e30).astype(jnp.float32))
        out = gq = gk = gv = None
        for side in sides:
            q_side = jnp.where(side, queries * jnp.bfloat16(0.125), zero)
            g_side = jnp.where(side, grads, zero)
            k_side = jnp.where(side, keys * jnp.bfloat16(0.125), zero)
            v_side = jnp.where(side, values, zero)
            top = None
            for slot in range(2 * TILES):
                span = slice(slot * TILE, (slot + 1) * TILE)
                score = times_transpose(keys[span], q_side) + biases[slot]
                score_ref[span, :] = score
                peak = jnp.max(score, axis=0, keepdims=True)
                top = peak if top is None else jnp.maximum(top, peak)
            total = inner = None
            for slot in range(2 * TILES):
                span = slice(slot * TILE, (slot + 1) * TILE)
                expo = jnp.exp(score_ref[span, :] - top)
                grad = times_transpose(values[span], g_side)
                score_ref[span, :] = expo
                grad_ref[span, :] = grad
                part = jnp.sum(expo, axis=0, keepdims=True)
                cross = jnp.sum(expo * grad, axis=0, keepdims=True)
                total = part if total is None else total + part
                inner = cross if inner is None else inner + cross
            scale = 1.0 / total
            inner = inner * scale
            probs, slopes = [], []
            for slot in range(2 * TILES):
                span = slice(slot * TILE, (slot + 1) * TILE)
                weight = score_ref[span, :] * scale
                probs.append(weight.astype(jnp.bfloat16))
                slopes.append((weight * (grad_ref[span, :] - inner)).astype(jnp.bfloat16))
            probs = jnp.concatenate(probs, 0)
            slopes = jnp.concatenate(slopes, 0)
            parts = (
                contract_rows(v_side, probs),
                contract_rows(k_side, slopes),
                dot(slopes, q_side),
                dot(probs, g_side),
            )
            if out is None:
                out, gq, gk, gv = parts
            else:
                out, gq, gk, gv = out + parts[0], gq + parts[1], gk + parts[2], gv + parts[3]
        out_ref[rows, :] = out.T.astype(jnp.bfloat16)
        gq_ref[rows, :] = gq.T.astype(jnp.bfloat16)
        own_ref[rows, k_span] = gk[:ROWS]
        own_ref[rows, v_span] = gv[:ROWS]
        border_k.append(gk[ROWS : ROWS + TILE].astype(jnp.bfloat16))
        border_v.append(gv[ROWS : ROWS + TILE].astype(jnp.bfloat16))
        for span, grad in ((k_span, gk), (v_span, gv)):
            sent = grad[ROWS + TILE :].astype(jnp.bfloat16)
            all_ref[far, span] = sent
            back1_ref[block, :, span] = sent[:TILE]
            back2_ref[block, :, span] = sent[TILE:]
    for block in range(2):
        other = pl.ds(
            pl.multiple_of((1 - block) * ROWS + ids_ref[1 - block, 0] * TILE, TILE), TILE
        )
        own_ref[other, k_span] += border_k[block].astype(jnp.float32)
        own_ref[other, v_span] += border_v[block].astype(jnp.float32)
    all_ref[:PAIR_ROWS, k_span] = own_ref[:, k_span].astype(jnp.bfloat16)
    all_ref[:PAIR_ROWS, v_span] = own_ref[:, v_span].astype(jnp.bfloat16)


def attention(part, mask, ids, q, kv, g, back):
    pair = 2 * HEAD
    steps = PART // pair

    def flat(rows, shift=0):
        return pl.BlockSpec((rows, pair), lambda j: (0, j + shift))

    def whole(*shape):
        return pl.BlockSpec(shape, lambda j: (0,) * len(shape))

    smem = pl.BlockSpec(memory_space=pltpu.SMEM)
    own, here = flat(PAIR_ROWS), flat(PAIR_ROWS, part * steps)
    shapes = [
        ((PAIR_ROWS, 2 * PART), jnp.float32),
        ((ALL_ROWS, 2 * PART), jnp.bfloat16),
    ]
    border = pl.BlockSpec((2, TILE, 2 * PART), lambda j: (0, 0, part))
    return pl.pallas_call(
        attention_kernel,
        grid=(steps,),
        in_specs=[
            smem, smem, here, flat(ALL_ROWS, part * steps),
            flat(ALL_ROWS, part * steps + HALF // pair), here,
        ]
        + [pl.BlockSpec(memory_space=pl.ANY)] * len(back),
        input_output_aliases={6 + index: 4 + index for index in range(len(back))},
        out_specs=[own, own] + [whole(*shape) for shape, _ in shapes] + [border] * 2,
        out_shape=[jax.ShapeDtypeStruct((PAIR_ROWS, PART), jnp.bfloat16)] * 2
        + [jax.ShapeDtypeStruct(*shape) for shape in shapes]
        + [jax.ShapeDtypeStruct((2, TILE, 2 * HALF), jnp.bfloat16)] * 2,
        scratch_shapes=[
            pltpu.VMEM((2 * ROWS, ROWS), jnp.float32),
            pltpu.VMEM((2 * ROWS, ROWS), jnp.float32),
        ],
        compiler_params=pltpu.CompilerParams(vmem_limit_bytes=56 * 1024 * 1024),
        cost_estimate=pl.CostEstimate(
            flops=8_000_000_000, bytes_accessed=8_000_000, transcendentals=2_500_000
        ),
        name="attention",
    )(mask, ids, q, kv, kv, g, *back)


def spread(value, axes, count):
    copies = jnp.broadcast_to(value[None], (count,) + value.shape)
    return lax.all_to_all(copies, axes, 0, 0, tiled=True)


def norm_kernel(gain_ref, *refs):
    out_ref = refs[-1]
    row = 0
    for ref in refs[:-1]:
        for at in range(0, ref.shape[0], TILE):
            wide = ref[at : at + TILE].astype(jnp.float32)
            square = jnp.mean(wide * wide, axis=1, keepdims=True) + epsilon
            inverse = lax.rsqrt(square)
            inverse = inverse * (1.5 - 0.5 * square * inverse * inverse)
            out_ref[row : row + TILE] = (wide * inverse * gain_ref[...]).astype(jnp.bfloat16)
            row += TILE


def norm_rows(gain, groups):
    rows = sum(group.shape[0] for group in groups)
    return pl.pallas_call(
        norm_kernel,
        out_shape=jax.ShapeDtypeStruct((rows, 1024), jnp.bfloat16),
        compiler_params=pltpu.CompilerParams(vmem_limit_bytes=56 * 1024 * 1024),
        cost_estimate=pl.CostEstimate(flops=6_000_000, bytes_accessed=5_000_000, transcendentals=1280),
        name="norm_rows",
    )(gain.reshape(1, 1024), *groups)


def norm(features, gain):
    wide = features.astype(jnp.float32)
    inverse = lax.rsqrt(jnp.mean(wide * wide, axis=1, keepdims=True) + epsilon)
    return wide, inverse, (wide * inverse * gain).astype(jnp.bfloat16)


def ring(distance):
    return [(z, (z + distance) % 8) for z in range(8)]


def row_block(value, index):
    return lax.dynamic_slice_in_dim(value, (index & 7) * TILE, TILE, 0)


def gather_ring(own, z, after):
    blocks = [(0, own)]
    up = down = own
    for step in range(1, 4):
        up = lax.ppermute(up, "z", ring(1))
        down = lax.ppermute(down, "z", ring(-1))
        if step == 2:
            _, after = lax.optimization_barrier(((up, down), after))
        blocks += [(-step, up), (step, down)]
    middle = own.shape[1] // 2
    up = lax.ppermute(up[:, :middle], "z", ring(1))
    down = lax.ppermute(down[:, middle:], "z", ring(-1))
    blocks.append((4, jnp.concatenate([up, down], 1)))
    out = jnp.zeros((1024, own.shape[1]), own.dtype)
    for distance, block in blocks:
        out = lax.dynamic_update_slice_in_dim(out, block, ((z + distance) & 7) * TILE, 0)
    return out, after


def terms_kernel(core_ref, rows_ref, kv_ref, q_ref, *refs):
    out_ref, out_term = refs[-1], None
    width = out_ref.shape[-1]
    terms = [
        contract_rows(rows_ref[...], kv_ref[...]),
        contract_rows(rows_ref[:PAIR_ROWS], q_ref[...]),
    ]
    if len(refs) > 1:
        *heads_refs, cot_ref, out_ref, out_term = refs
        place = (pl.program_id(0) + 2 * core_ref[0]) & 3
        for index, heads_ref in enumerate(heads_refs):

            @pl.when(place == index)
            def _():
                if index < 2:
                    out_term[...] = contract_rows(heads_ref[...], cot_ref[...])
                else:
                    out_term[...] = contract_rows(
                        heads_ref[:ROWS], cot_ref[ROWS:]
                    ) + contract_rows(heads_ref[ROWS:], cot_ref[:ROWS])

        width = out_ref.shape[-1]
        terms.append(out_term[...])
    terms = jnp.concatenate([term.astype(jnp.bfloat16) for term in terms], 1)
    for block in range(2):
        for piece in range(8):
            row = block * TILE + piece * SLAB
            for which in range(2):
                out_ref[piece // 4, piece % 4, which, block] = terms[
                    row : row + SLAB, which * width : (which + 1) * width
                ]


def weight_terms(core, rows, grad_kv, grad_q, heads=(), cot=None):
    def whole(value):
        return pl.BlockSpec(value.shape, lambda j, c: (0, 0))

    operands = [rows, grad_kv, grad_q]
    width = 3 * PART // 2
    scratch = []
    if heads:
        operands += [*heads, cot]
        width += HALF // 2
        scratch = [pltpu.VMEM((2 * TILE, HALF), jnp.float32)]
    pieces = pl.pallas_call(
        terms_kernel,
        grid_spec=pltpu.PrefetchScalarGridSpec(
            num_scalar_prefetch=1,
            grid=(4,),
            in_specs=[pl.BlockSpec((ALL_ROWS, 2 * TILE), lambda j, c: (0, j))]
            + [whole(value) for value in operands[1:]],
            out_specs=pl.BlockSpec((2, 4, 2, 2, SLAB, width), lambda j, c: (0, 0, 0, j, 0, 0)),
            scratch_shapes=scratch,
        ),
        out_shape=jax.ShapeDtypeStruct((2, 4, 2, 8, SLAB, width), jnp.bfloat16),
        compiler_params=pltpu.CompilerParams(vmem_limit_bytes=56 * 1024 * 1024),
        cost_estimate=pl.CostEstimate(
            flops=2_000_000_000, bytes_accessed=8_000_000, transcendentals=0
        ),
        name="weight_terms",
    )(core.astype(jnp.int32).reshape(1), *operands)
    return pieces.reshape(16, 8, SLAB, width)


def row_gradient_kernel(ids_ref, weight_ref, *refs):
    *refs, first_ref, second_ref, mine_ref, theirs_ref = refs
    for block, out_ref in enumerate((mine_ref, theirs_ref)):
        total = None
        for step in range(HALF // PART):
            own_ref, q_ref = refs[2 * step : 2 * step + 2]
            columns = slice(step * 2 * PART, (step + 1) * 2 * PART)
            tiles = []
            for tile in range(TILES):
                row = block * ROWS + tile * TILE
                grad = own_ref[row : row + TILE]
                for slot, back_ref in enumerate((first_ref, second_ref)):
                    back = back_ref[block, :, columns].astype(jnp.float32)
                    grad += jnp.where(ids_ref[block, slot + 1] == tile, back, 0.0)
                tiles.append(grad.astype(jnp.bfloat16))
            tiles = jnp.concatenate(tiles, 0)
            grads = (tiles[:, :PART], tiles[:, PART:], q_ref[block * ROWS : (block + 1) * ROWS])
            for which, grad in enumerate(grads):
                at = which * HALF + step * PART
                part = times_transpose(grad, weight_ref[:, at : at + PART])
                total = part if total is None else total + part
        out_ref[...] = total


def row_gradients(ids, weight, grad_own, grad_q, returned):
    operands = [ids, weight]
    for pair in zip(grad_own, grad_q):
        operands += pair
    operands += returned
    vmem = pl.BlockSpec(memory_space=pltpu.VMEM)
    return pl.pallas_call(
        row_gradient_kernel,
        in_specs=[pl.BlockSpec(memory_space=pltpu.SMEM)] + [vmem] * (len(operands) - 1),
        out_shape=[jax.ShapeDtypeStruct((ROWS, 1024), jnp.float32)] * 2,
        compiler_params=pltpu.CompilerParams(vmem_limit_bytes=56 * 1024 * 1024),
        cost_estimate=pl.CostEstimate(
            flops=2_500_000_000, bytes_accessed=16_000_000, transcendentals=0
        ),
        name="row_gradients",
    )(*operands)


QUERY_COLUMNS = ((1, 128, 384), (0, 896, 1024), (1, 384, 512))
KEY_COLUMNS = ((0, 0, 256), (0, 384, 640))
VALUE_COLUMNS = ((0, 256, 384), (1, 0, 128), (0, 640, 896))
OUT_COLUMNS = ((1, 512, 1024),)


def unpack_kernel(in_ref, *out_refs):
    columns = (QUERY_COLUMNS, KEY_COLUMNS, VALUE_COLUMNS, OUT_COLUMNS)
    for out_ref, spans in zip(out_refs, columns):
        for y in range(4):
            rows = slice(y * SLAB, (y + 1) * SLAB)
            for side in range(2):
                at = side * HALF
                for which, start, stop in spans:
                    value = in_ref[(y * 2 + which) * 2 + side, :, start:stop]
                    out_ref[rows, at : at + stop - start] = value.astype(jnp.float32)
                    at += stop - start


def unpack(gathered):
    return pl.pallas_call(
        unpack_kernel,
        out_shape=[jax.ShapeDtypeStruct((64, 1024), jnp.float32)] * 4,
        name="unpack",
    )(gathered)


def reduce_arrived(arrived):
    return jnp.sum(arrived.astype(jnp.float32), axis=0).astype(jnp.bfloat16)


def local(
    node_features, norm_gain, query_weight, key_weight, value_weight, out_weight,
    cotangent, pair_mask, border_ids,
):
    core, z, xl = (lax.axis_index(axis) for axis in ("core", "z", "xl"))
    plane = lax.axis_index("y") * 2 + lax.axis_index("xh")
    routes = (("xh", SWAP), ("y", [(0, 1), (1, 0), (2, 3), (3, 2)]))

    def half_of(value, which, axis=1):
        return lax.dynamic_slice_in_dim(value, which * HALF, HALF, axis)

    def both(value):
        return jnp.concatenate([value, swap_core(value)], 0)

    first = jnp.concatenate(
        [half_of(weight, core) for weight in (key_weight, value_weight, query_weight)], 1
    )
    piece = lax.dynamic_slice_in_dim(half_of(out_weight, core), plane * 8, 8, 0)
    fetched = spread(piece, "z", 8)
    other = lax.ppermute(first, "xl", SWAP)
    own = jnp.concatenate([jnp.where(xl == 0, first, other), jnp.where(xl == 0, other, first)], 0)
    own, features, border_ids = lax.optimization_barrier((own, node_features, border_ids))
    border = [
        lax.ppermute(
            lax.dynamic_slice_in_dim(features, border_ids[0, bit + 1] * TILE, TILE, 0),
            axis,
            route,
        )
        for bit, (axis, route) in enumerate(routes)
    ]
    weights, fetched = gather_ring(own, z, fetched)
    fetched = spread(fetched, PLANE, 16)
    out_half = fetched.transpose(1, 0, 2, 3).reshape(1024, HALF)

    plan = both(jnp.concatenate([pair_mask, jnp.broadcast_to(border_ids, (TILES, TILES))], 1))
    mask = plan[:, : 2 * TILES]
    ids = plan[:: TILES, 2 * TILES :]
    normed = norm_rows(
        norm_gain,
        [features, swap_core(features)] + border + [swap_core(tile) for tile in border],
    )
    cotangents = both(cotangent)
    cot_mine, cot_other = half_of(cotangents, core), half_of(cotangents, 1 - core)

    out_mine = half_of(out_half, core, 0)
    out_other = half_of(out_half, 1 - core, 0)
    out_swapped = swap_core(out_other)
    grad_attended = (
        times_transpose(cot_mine, out_mine) + times_transpose(cot_other, out_swapped)
    ).astype(jnp.bfloat16)

    attended, swapped, grad_q, grad_own, parts, back = ([] for _ in range(6))
    kv = dot(normed, weights[:, : 2 * HALF]).astype(jnp.bfloat16)
    q = dot(normed[:PAIR_ROWS], weights[:, 2 * HALF :]).astype(jnp.bfloat16)
    for step in range(HALF // PART):
        out, gq, own_kv, gkv, *back = attention(step, mask, ids, q, kv, grad_attended, back)
        attended.append(out)
        swapped.append(swap_core(out))
        grad_q.append(gq)
        grad_own.append(own_kv)
        if step == HALF // PART - 1:
            terms = weight_terms(core, normed, gkv, gq, attended + swapped, cot_mine)
            returned = [lax.ppermute(tiles, *to) for tiles, to in zip(back, routes)]
            terms, attended, swapped, grad_q, returned = lax.optimization_barrier(
                (terms, attended, swapped, grad_q, returned)
            )
        else:
            terms = weight_terms(core, normed, gkv, gq)
            terms, grad_attended = lax.optimization_barrier((terms, grad_attended))
        parts.append(reduce_arrived(lax.all_to_all(terms, PLANE, 0, 0, tiled=True)))
    part = jnp.concatenate(parts, -1)
    swapped = [jnp.concatenate([value[ROWS:], value[:ROWS]], 0) for value in swapped]
    update = dot(
        jnp.concatenate(attended + swapped, 1), jnp.concatenate([out_mine, out_other], 0)
    ).astype(jnp.bfloat16)
    update_mine, update_other = update[:ROWS], swap_core(update[ROWS:])
    layer_update = jnp.concatenate(
        [
            jnp.where(core == 0, update_mine, update_other),
            jnp.where(core == 0, update_other, update_mine),
        ],
        1,
    )

    grad_mine, grad_theirs = row_gradients(ids, weights, grad_own, grad_q, returned)
    scaled = (grad_mine + swap_core(grad_theirs)) * norm_gain
    wide, inverse, _ = norm(node_features, norm_gain)
    inner_mean = jnp.mean(scaled * wide, axis=1, keepdims=True)
    node_gradient = (inverse * scaled - wide * inverse**3 * inner_mean).astype(jnp.bfloat16)
    part, layer_update = lax.optimization_barrier((part, layer_update))
    total = reduce_arrived(lax.all_to_all(part, "z", 0, 0, tiled=True))
    weight_gradients = unpack(spread(total, FACE, 16))

    return layer_update, node_gradient, *weight_gradients


def solution(mesh):
    fine = Mesh(mesh.devices.reshape(4, 2, 2, 8, 2), NODES)
    rows = P(NODES, None)
    weight = P(FSDP, None)
    return jax.shard_map(
        local,
        mesh=fine,
        in_specs=(rows, P(), weight, weight, weight, weight, rows, rows, rows),
        out_specs=(rows, rows, weight, weight, weight, weight),
        check_vma=False,
    )
```

```python
import functools

import jax
import jax.numpy as jnp
from jax import lax
from jax.experimental import pallas as pl
from jax.experimental.pallas import tpu as pltpu
from jax.sharding import Mesh, PartitionSpec as P


TILE = 128
TILES = 3
ROWS = TILE * TILES
PAIR_ROWS = 2 * ROWS
ALL_ROWS = PAIR_ROWS + 4 * TILE
HEAD = 64
HALF = 512
PART = 256
SLAB = 16
epsilon = 1e-06

FACE = ("y", "xh", "core")
PLANE = ("xl", "y", "xh")
FSDP = ("z", "xl")
NODES = FACE + FSDP
SWAP = [(0, 1), (1, 0)]


def contract_rows(left, right):
    return lax.dot_general(
        left, right, (((0,), (0,)), ((), ())), preferred_element_type=jnp.float32
    )


def times_transpose(left, right):
    return lax.dot_general(
        left, right, (((1,), (1,)), ((), ())), preferred_element_type=jnp.float32
    )


def dot(left, right):
    return jnp.dot(left, right, preferred_element_type=jnp.float32)


def swap_core(value):
    return lax.ppermute(value, "core", SWAP)


def attention_kernel(
    mask_ref, ids_ref, q_ref, k_ref, v_ref, g_ref, *refs
):
    out_ref, gq_ref, own_ref, all_ref, back1_ref, back2_ref, score_ref, grad_ref = refs[-8:]
    lane = lax.broadcasted_iota(jnp.int32, (1, 2 * HEAD), 1)
    column = lax.broadcasted_iota(jnp.int32, (1, ROWS), 1)
    sides = [(lane < HEAD), (lane >= HEAD)]
    zero = jnp.zeros((), jnp.bfloat16)
    step = pl.program_id(0) * 2 * HEAD
    k_span = pl.ds(pl.multiple_of(step, 2 * HEAD), 2 * HEAD)
    v_span = pl.ds(pl.multiple_of(PART + step, 2 * HEAD), 2 * HEAD)
    border_k, border_v = [], []
    for block in range(2):
        rows = pl.ds(block * ROWS, ROWS)
        other = pl.ds(
            pl.multiple_of((1 - block) * ROWS + ids_ref[1 - block, 0] * TILE, TILE), TILE
        )
        far = slice(PAIR_ROWS + block * 2 * TILE, PAIR_ROWS + (block + 1) * 2 * TILE)
        keys = jnp.concatenate([k_ref[rows, :], k_ref[other, :], k_ref[far, :]], 0)
        values = jnp.concatenate([v_ref[rows, :], v_ref[other, :], v_ref[far, :]], 0)
        queries = q_ref[rows, :]
        grads = g_ref[rows, :]
        biases = []
        for slot in range(2 * TILES):
            parts = [mask_ref[block * TILES + t, slot] for t in range(TILES)]
            live = jnp.where(
                column < TILE, parts[0], jnp.where(column < 2 * TILE, parts[1], parts[2])
            )
            biases.append(jnp.where(live > 0, 0.0, -1e30).astype(jnp.float32))
        out = gq = gk = gv = None
        for side in sides:
            q_side = jnp.where(side, queries * jnp.bfloat16(0.125), zero)
            g_side = jnp.where(side, grads, zero)
            k_side = jnp.where(side, keys * jnp.bfloat16(0.125), zero)
            v_side = jnp.where(side, values, zero)
            top = None
            for slot in range(2 * TILES):
                span = slice(slot * TILE, (slot + 1) * TILE)
                score = times_transpose(keys[span], q_side) + biases[slot]
                score_ref[span, :] = score
                peak = jnp.max(score, axis=0, keepdims=True)
                top = peak if top is None else jnp.maximum(top, peak)
            total = inner = None
            for slot in range(2 * TILES):
                span = slice(slot * TILE, (slot + 1) * TILE)
                expo = jnp.exp(score_ref[span, :] - top)
                grad = times_transpose(values[span], g_side)
                score_ref[span, :] = expo
                grad_ref[span, :] = grad
                part = jnp.sum(expo, axis=0, keepdims=True)
                cross = jnp.sum(expo * grad, axis=0, keepdims=True)
                total = part if total is None else total + part
                inner = cross if inner is None else inner + cross
            scale = 1.0 / total
            inner = inner * scale
            probs, slopes = [], []
            for slot in range(2 * TILES):
                span = slice(slot * TILE, (slot + 1) * TILE)
                weight = score_ref[span, :] * scale
                probs.append(weight.astype(jnp.bfloat16))
                slopes.append((weight * (grad_ref[span, :] - inner)).astype(jnp.bfloat16))
            probs = jnp.concatenate(probs, 0)
            slopes = jnp.concatenate(slopes, 0)
            parts = (
                contract_rows(v_side, probs),
                contract_rows(k_side, slopes),
                dot(slopes, q_side),
                dot(probs, g_side),
            )
            if out is None:
                out, gq, gk, gv = parts
            else:
                out, gq, gk, gv = out + parts[0], gq + parts[1], gk + parts[2], gv + parts[3]
        out_ref[rows, :] = out.T.astype(jnp.bfloat16)
        gq_ref[rows, :] = gq.T.astype(jnp.bfloat16)
        own_ref[rows, k_span] = gk[:ROWS]
        own_ref[rows, v_span] = gv[:ROWS]
        border_k.append(gk[ROWS : ROWS + TILE].astype(jnp.bfloat16))
        border_v.append(gv[ROWS : ROWS + TILE].astype(jnp.bfloat16))
        for span, grad in ((k_span, gk), (v_span, gv)):
            sent = grad[ROWS + TILE :].astype(jnp.bfloat16)
            all_ref[far, span] = sent
            back1_ref[block, :, span] = sent[:TILE]
            back2_ref[block, :, span] = sent[TILE:]
    for block in range(2):
        other = pl.ds(
            pl.multiple_of((1 - block) * ROWS + ids_ref[1 - block, 0] * TILE, TILE), TILE
        )
        own_ref[other, k_span] += border_k[block].astype(jnp.float32)
        own_ref[other, v_span] += border_v[block].astype(jnp.float32)
    all_ref[:PAIR_ROWS, k_span] = own_ref[:, k_span].astype(jnp.bfloat16)
    all_ref[:PAIR_ROWS, v_span] = own_ref[:, v_span].astype(jnp.bfloat16)


def attention(part, mask, ids, q, kv, g, back):
    pair = 2 * HEAD
    steps = PART // pair

    def flat(rows, shift=0):
        return pl.BlockSpec((rows, pair), lambda j: (0, j + shift))

    def whole(*shape):
        return pl.BlockSpec(shape, lambda j: (0,) * len(shape))

    smem = pl.BlockSpec(memory_space=pltpu.SMEM)
    own, here = flat(PAIR_ROWS), flat(PAIR_ROWS, part * steps)
    shapes = [
        ((PAIR_ROWS, 2 * PART), jnp.float32),
        ((ALL_ROWS, 2 * PART), jnp.bfloat16),
    ]
    border = pl.BlockSpec((2, TILE, 2 * PART), lambda j: (0, 0, part))
    return pl.pallas_call(
        attention_kernel,
        grid=(steps,),
        in_specs=[
            smem, smem, here, flat(ALL_ROWS, part * steps),
            flat(ALL_ROWS, part * steps + HALF // pair), here,
        ]
        + [pl.BlockSpec(memory_space=pl.ANY)] * len(back),
        input_output_aliases={6 + index: 4 + index for index in range(len(back))},
        out_specs=[own, own] + [whole(*shape) for shape, _ in shapes] + [border] * 2,
        out_shape=[jax.ShapeDtypeStruct((PAIR_ROWS, PART), jnp.bfloat16)] * 2
        + [jax.ShapeDtypeStruct(*shape) for shape in shapes]
        + [jax.ShapeDtypeStruct((2, TILE, 2 * HALF), jnp.bfloat16)] * 2,
        scratch_shapes=[
            pltpu.VMEM((2 * ROWS, ROWS), jnp.float32),
            pltpu.VMEM((2 * ROWS, ROWS), jnp.float32),
        ],
        compiler_params=pltpu.CompilerParams(vmem_limit_bytes=40 * 1024 * 1024),
        cost_estimate=pl.CostEstimate(
            flops=8_000_000_000, bytes_accessed=8_000_000, transcendentals=2_500_000
        ),
        name="attention",
    )(mask, ids, q, kv, kv, g, *back)


def spread(value, axes, count):
    copies = jnp.broadcast_to(value[None], (count,) + value.shape)
    return lax.all_to_all(copies, axes, 0, 0, tiled=True)


def norm_kernel(gain_ref, *refs):
    out_ref = refs[-1]
    row = 0
    for ref in refs[:-1]:
        for at in range(0, ref.shape[0], TILE):
            wide = ref[at : at + TILE].astype(jnp.float32)
            square = jnp.mean(wide * wide, axis=1, keepdims=True) + epsilon
            inverse = lax.rsqrt(square)
            inverse = inverse * (1.5 - 0.5 * square * inverse * inverse)
            out_ref[row : row + TILE] = (wide * inverse * gain_ref[...]).astype(jnp.bfloat16)
            row += TILE


def norm_rows(gain, groups):
    rows = sum(group.shape[0] for group in groups)
    return pl.pallas_call(
        norm_kernel,
        out_shape=jax.ShapeDtypeStruct((rows, 1024), jnp.bfloat16),
        compiler_params=pltpu.CompilerParams(vmem_limit_bytes=40 * 1024 * 1024),
        cost_estimate=pl.CostEstimate(flops=6_000_000, bytes_accessed=5_000_000, transcendentals=1280),
        name="norm_rows",
    )(gain.reshape(1, 1024), *groups)


def norm(features, gain):
    wide = features.astype(jnp.float32)
    inverse = lax.rsqrt(jnp.mean(wide * wide, axis=1, keepdims=True) + epsilon)
    return wide, inverse, (wide * inverse * gain).astype(jnp.bfloat16)


def ring(distance):
    return [(z, (z + distance) % 8) for z in range(8)]


def row_block(value, index):
    return lax.dynamic_slice_in_dim(value, (index & 7) * TILE, TILE, 0)


def gather_ring(own, z):
    blocks = [(0, own)]
    up = down = own
    for step in range(1, 4):
        up = lax.ppermute(up, "z", ring(1))
        down = lax.ppermute(down, "z", ring(-1))
        blocks += [(-step, up), (step, down)]
    middle = own.shape[1] // 2
    up = lax.ppermute(up[:, :middle], "z", ring(1))
    down = lax.ppermute(down[:, middle:], "z", ring(-1))
    blocks.append((4, jnp.concatenate([up, down], 1)))
    out = jnp.zeros((1024, own.shape[1]), own.dtype)
    for distance, block in blocks:
        out = lax.dynamic_update_slice_in_dim(out, block, ((z + distance) & 7) * TILE, 0)
    return out


def terms_kernel(core_ref, rows_ref, kv_ref, q_ref, *refs):
    out_ref, out_term = refs[-1], None
    width = out_ref.shape[-1]
    terms = [
        contract_rows(rows_ref[...], kv_ref[...]),
        contract_rows(rows_ref[:PAIR_ROWS], q_ref[...]),
    ]
    if len(refs) > 1:
        *heads_refs, cot_ref, out_ref, out_term = refs
        place = (pl.program_id(0) + 2 * core_ref[0]) & 3
        for index, heads_ref in enumerate(heads_refs):

            @pl.when(place == index)
            def _():
                if index < 2:
                    out_term[...] = contract_rows(heads_ref[...], cot_ref[...])
                else:
                    out_term[...] = contract_rows(
                        heads_ref[:ROWS], cot_ref[ROWS:]
                    ) + contract_rows(heads_ref[ROWS:], cot_ref[:ROWS])

        width = out_ref.shape[-1]
        terms.append(out_term[...])
    terms = jnp.concatenate([term.astype(jnp.bfloat16) for term in terms], 1)
    for block in range(2):
        for piece in range(8):
            row = block * TILE + piece * SLAB
            for which in range(2):
                out_ref[piece // 4, piece % 4, which, block] = terms[
                    row : row + SLAB, which * width : (which + 1) * width
                ]


def weight_terms(core, rows, grad_kv, grad_q, heads=(), cot=None):
    def whole(value):
        return pl.BlockSpec(value.shape, lambda j, c: (0, 0))

    operands = [rows, grad_kv, grad_q]
    width = 3 * PART // 2
    scratch = []
    if heads:
        operands += [*heads, cot]
        width += HALF // 2
        scratch = [pltpu.VMEM((2 * TILE, HALF), jnp.float32)]
    pieces = pl.pallas_call(
        terms_kernel,
        grid_spec=pltpu.PrefetchScalarGridSpec(
            num_scalar_prefetch=1,
            grid=(4,),
            in_specs=[pl.BlockSpec((ALL_ROWS, 2 * TILE), lambda j, c: (0, j))]
            + [whole(value) for value in operands[1:]],
            out_specs=pl.BlockSpec((2, 4, 2, 2, SLAB, width), lambda j, c: (0, 0, 0, j, 0, 0)),
            scratch_shapes=scratch,
        ),
        out_shape=jax.ShapeDtypeStruct((2, 4, 2, 8, SLAB, width), jnp.bfloat16),
        compiler_params=pltpu.CompilerParams(vmem_limit_bytes=40 * 1024 * 1024),
        cost_estimate=pl.CostEstimate(
            flops=2_000_000_000, bytes_accessed=8_000_000, transcendentals=0
        ),
        name="weight_terms",
    )(core.astype(jnp.int32).reshape(1), *operands)
    return pieces.reshape(16, 8, SLAB, width)


def row_gradient_kernel(ids_ref, weight_ref, *refs):
    *refs, first_ref, second_ref, mine_ref, theirs_ref = refs
    for block, out_ref in enumerate((mine_ref, theirs_ref)):
        total = None
        for step in range(HALF // PART):
            own_ref, q_ref = refs[2 * step : 2 * step + 2]
            columns = slice(step * 2 * PART, (step + 1) * 2 * PART)
            tiles = []
            for tile in range(TILES):
                row = block * ROWS + tile * TILE
                grad = own_ref[row : row + TILE]
                for slot, back_ref in enumerate((first_ref, second_ref)):
                    back = back_ref[block, :, columns].astype(jnp.float32)
                    grad += jnp.where(ids_ref[block, slot + 1] == tile, back, 0.0)
                tiles.append(grad.astype(jnp.bfloat16))
            tiles = jnp.concatenate(tiles, 0)
            grads = (tiles[:, :PART], tiles[:, PART:], q_ref[block * ROWS : (block + 1) * ROWS])
            for which, grad in enumerate(grads):
                at = which * HALF + step * PART
                part = times_transpose(grad, weight_ref[:, at : at + PART])
                total = part if total is None else total + part
        out_ref[...] = total


def row_gradients(ids, weight, grad_own, grad_q, returned):
    operands = [ids, weight]
    for pair in zip(grad_own, grad_q):
        operands += pair
    operands += returned
    vmem = pl.BlockSpec(memory_space=pltpu.VMEM)
    return pl.pallas_call(
        row_gradient_kernel,
        in_specs=[pl.BlockSpec(memory_space=pltpu.SMEM)] + [vmem] * (len(operands) - 1),
        out_shape=[jax.ShapeDtypeStruct((ROWS, 1024), jnp.float32)] * 2,
        compiler_params=pltpu.CompilerParams(vmem_limit_bytes=40 * 1024 * 1024),
        cost_estimate=pl.CostEstimate(
            flops=2_500_000_000, bytes_accessed=16_000_000, transcendentals=0
        ),
        name="row_gradients",
    )(*operands)


QUERY_COLUMNS = ((1, 128, 384), (0, 896, 1024), (1, 384, 512))
KEY_COLUMNS = ((0, 0, 256), (0, 384, 640))
VALUE_COLUMNS = ((0, 256, 384), (1, 0, 128), (0, 640, 896))
OUT_COLUMNS = ((1, 512, 1024),)


def unpack_kernel(in_ref, *out_refs):
    columns = (QUERY_COLUMNS, KEY_COLUMNS, VALUE_COLUMNS, OUT_COLUMNS)
    for out_ref, spans in zip(out_refs, columns):
        for y in range(4):
            rows = slice(y * SLAB, (y + 1) * SLAB)
            for side in range(2):
                at = side * HALF
                for which, start, stop in spans:
                    value = in_ref[(y * 2 + which) * 2 + side, :, start:stop]
                    out_ref[rows, at : at + stop - start] = value.astype(jnp.float32)
                    at += stop - start


def unpack(gathered):
    return pl.pallas_call(
        unpack_kernel,
        out_shape=[jax.ShapeDtypeStruct((64, 1024), jnp.float32)] * 4,
        name="unpack",
    )(gathered)


def reduce_arrived(arrived):
    return jnp.sum(arrived.astype(jnp.float32), axis=0).astype(jnp.bfloat16)


def local(
    node_features, norm_gain, query_weight, key_weight, value_weight, out_weight,
    cotangent, pair_mask, border_ids,
):
    core, z, xl = (lax.axis_index(axis) for axis in ("core", "z", "xl"))
    routes = (("xh", SWAP), ("y", [(0, 1), (1, 0), (2, 3), (3, 2)]))

    def half_of(value, which, axis=1):
        return lax.dynamic_slice_in_dim(value, which * HALF, HALF, axis)

    def both(value):
        return jnp.concatenate([value, swap_core(value)], 0)

    first = jnp.concatenate(
        [half_of(weight, core) for weight in (key_weight, value_weight, query_weight, out_weight)],
        1,
    )
    other = lax.ppermute(first, "xl", SWAP)
    own = jnp.concatenate([jnp.where(xl == 0, first, other), jnp.where(xl == 0, other, first)], 0)
    own, features, border_ids = lax.optimization_barrier((own, node_features, border_ids))
    border = [
        lax.ppermute(
            lax.dynamic_slice_in_dim(features, border_ids[0, bit + 1] * TILE, TILE, 0),
            axis,
            route,
        )
        for bit, (axis, route) in enumerate(routes)
    ]
    weights = gather_ring(own, z)
    out_half = weights[:, 3 * HALF :]

    plan = both(jnp.concatenate([pair_mask, jnp.broadcast_to(border_ids, (TILES, TILES))], 1))
    mask = plan[:, : 2 * TILES]
    ids = plan[:: TILES, 2 * TILES :]
    normed = norm_rows(
        norm_gain,
        [features, swap_core(features)] + border + [swap_core(tile) for tile in border],
    )
    cotangents = both(cotangent)
    cot_mine, cot_other = half_of(cotangents, core), half_of(cotangents, 1 - core)

    out_mine = half_of(out_half, core, 0)
    out_other = half_of(out_half, 1 - core, 0)
    out_swapped = swap_core(out_other)
    grad_attended = (
        times_transpose(cot_mine, out_mine) + times_transpose(cot_other, out_swapped)
    ).astype(jnp.bfloat16)

    attended, swapped, grad_q, grad_own, parts, back = ([] for _ in range(6))
    kv = dot(normed, weights[:, : 2 * HALF]).astype(jnp.bfloat16)
    q = dot(normed[:PAIR_ROWS], weights[:, 2 * HALF : 3 * HALF]).astype(jnp.bfloat16)
    for step in range(HALF // PART):
        out, gq, own_kv, gkv, *back = attention(step, mask, ids, q, kv, grad_attended, back)
        attended.append(out)
        swapped.append(swap_core(out))
        grad_q.append(gq)
        grad_own.append(own_kv)
        if step == HALF // PART - 1:
            terms = weight_terms(core, normed, gkv, gq, attended + swapped, cot_mine)
            returned = [lax.ppermute(tiles, *to) for tiles, to in zip(back, routes)]
            terms, attended, swapped, grad_q, returned = lax.optimization_barrier(
                (terms, attended, swapped, grad_q, returned)
            )
        else:
            terms = weight_terms(core, normed, gkv, gq)
            terms, grad_attended = lax.optimization_barrier((terms, grad_attended))
        parts.append(reduce_arrived(lax.all_to_all(terms, PLANE, 0, 0, tiled=True)))
    part = jnp.concatenate(parts, -1)
    swapped = [jnp.concatenate([value[ROWS:], value[:ROWS]], 0) for value in swapped]
    update = dot(
        jnp.concatenate(attended + swapped, 1), jnp.concatenate([out_mine, out_other], 0)
    ).astype(jnp.bfloat16)
    update_mine, update_other = update[:ROWS], swap_core(update[ROWS:])
    layer_update = jnp.concatenate(
        [
            jnp.where(core == 0, update_mine, update_other),
            jnp.where(core == 0, update_other, update_mine),
        ],
        1,
    )

    grad_mine, grad_theirs = row_gradients(ids, weights, grad_own, grad_q, returned)
    scaled = (grad_mine + swap_core(grad_theirs)) * norm_gain
    wide, inverse, _ = norm(node_features, norm_gain)
    inner_mean = jnp.mean(scaled * wide, axis=1, keepdims=True)
    node_gradient = (inverse * scaled - wide * inverse**3 * inner_mean).astype(jnp.bfloat16)
    part, layer_update = lax.optimization_barrier((part, layer_update))
    total = reduce_arrived(lax.all_to_all(part, "z", 0, 0, tiled=True))
    weight_gradients = unpack(spread(total, FACE, 16))

    return layer_update, node_gradient, *weight_gradients


def solution(mesh):
    fine = Mesh(mesh.devices.reshape(4, 2, 2, 8, 2), NODES)
    rows = P(NODES, None)
    weight = P(FSDP, None)
    return jax.shard_map(
        local,
        mesh=fine,
        in_specs=(rows, P(), weight, weight, weight, weight, rows, rows, rows),
        out_specs=(rows, rows, weight, weight, weight, weight),
        check_vma=False,
    )
```

```python
import functools

import jax
import jax.numpy as jnp
from jax import lax
from jax.experimental import pallas as pl
from jax.experimental.pallas import tpu as pltpu
from jax.sharding import Mesh, PartitionSpec as P


TILE = 128
TILES = 3
ROWS = TILE * TILES
PAIR_ROWS = 2 * ROWS
ALL_ROWS = PAIR_ROWS + 4 * TILE
HEAD = 64
HALF = 512
PART = 256
SLAB = 16
epsilon = 1e-06

FACE = ("y", "xh", "core")
PLANE = ("xl", "y", "xh")
FSDP = ("z", "xl")
NODES = FACE + FSDP
SWAP = [(0, 1), (1, 0)]


def contract_rows(left, right):
    return lax.dot_general(
        left, right, (((0,), (0,)), ((), ())), preferred_element_type=jnp.float32
    )


def times_transpose(left, right):
    return lax.dot_general(
        left, right, (((1,), (1,)), ((), ())), preferred_element_type=jnp.float32
    )


def dot(left, right):
    return jnp.dot(left, right, preferred_element_type=jnp.float32)


def swap_core(value):
    return lax.ppermute(value, "core", SWAP)


def attention_kernel(
    mask_ref, ids_ref, q_ref, k_ref, v_ref, g_ref, *refs
):
    out_ref, gq_ref, own_ref, all_ref, back1_ref, back2_ref, score_ref, grad_ref = refs[-8:]
    lane = lax.broadcasted_iota(jnp.int32, (1, 2 * HEAD), 1)
    column = lax.broadcasted_iota(jnp.int32, (1, ROWS), 1)
    sides = [(lane < HEAD), (lane >= HEAD)]
    zero = jnp.zeros((), jnp.bfloat16)
    step = pl.program_id(0) * 2 * HEAD
    k_span = pl.ds(pl.multiple_of(step, 2 * HEAD), 2 * HEAD)
    v_span = pl.ds(pl.multiple_of(PART + step, 2 * HEAD), 2 * HEAD)
    border_k, border_v = [], []
    for block in range(2):
        rows = pl.ds(block * ROWS, ROWS)
        other = pl.ds(
            pl.multiple_of((1 - block) * ROWS + ids_ref[1 - block, 0] * TILE, TILE), TILE
        )
        far = slice(PAIR_ROWS + block * 2 * TILE, PAIR_ROWS + (block + 1) * 2 * TILE)
        keys = jnp.concatenate([k_ref[rows, :], k_ref[other, :], k_ref[far, :]], 0)
        values = jnp.concatenate([v_ref[rows, :], v_ref[other, :], v_ref[far, :]], 0)
        queries = q_ref[rows, :]
        grads = g_ref[rows, :]
        biases = []
        for slot in range(2 * TILES):
            parts = [mask_ref[block * TILES + t, slot] for t in range(TILES)]
            live = jnp.where(
                column < TILE, parts[0], jnp.where(column < 2 * TILE, parts[1], parts[2])
            )
            biases.append(jnp.where(live > 0, 0.0, -1e30).astype(jnp.float32))
        out = gq = gk = gv = None
        for side in sides:
            q_side = jnp.where(side, queries * jnp.bfloat16(0.125), zero)
            g_side = jnp.where(side, grads, zero)
            k_side = jnp.where(side, keys * jnp.bfloat16(0.125), zero)
            v_side = jnp.where(side, values, zero)
            top = None
            for slot in range(2 * TILES):
                span = slice(slot * TILE, (slot + 1) * TILE)
                score = times_transpose(keys[span], q_side) + biases[slot]
                score_ref[span, :] = score
                peak = jnp.max(score, axis=0, keepdims=True)
                top = peak if top is None else jnp.maximum(top, peak)
            total = inner = None
            for slot in range(2 * TILES):
                span = slice(slot * TILE, (slot + 1) * TILE)
                expo = jnp.exp(score_ref[span, :] - top)
                grad = times_transpose(values[span], g_side)
                score_ref[span, :] = expo
                grad_ref[span, :] = grad
                part = jnp.sum(expo, axis=0, keepdims=True)
                cross = jnp.sum(expo * grad, axis=0, keepdims=True)
                total = part if total is None else total + part
                inner = cross if inner is None else inner + cross
            scale = 1.0 / total
            inner = inner * scale
            probs, slopes = [], []
            for slot in range(2 * TILES):
                span = slice(slot * TILE, (slot + 1) * TILE)
                weight = score_ref[span, :] * scale
                probs.append(weight.astype(jnp.bfloat16))
                slopes.append((weight * (grad_ref[span, :] - inner)).astype(jnp.bfloat16))
            probs = jnp.concatenate(probs, 0)
            slopes = jnp.concatenate(slopes, 0)
            parts = (
                contract_rows(v_side, probs),
                contract_rows(k_side, slopes),
                dot(slopes, q_side),
                dot(probs, g_side),
            )
            if out is None:
                out, gq, gk, gv = parts
            else:
                out, gq, gk, gv = out + parts[0], gq + parts[1], gk + parts[2], gv + parts[3]
        out_ref[rows, :] = out.T.astype(jnp.bfloat16)
        gq_ref[rows, :] = gq.T.astype(jnp.bfloat16)
        own_ref[rows, k_span] = gk[:ROWS]
        own_ref[rows, v_span] = gv[:ROWS]
        border_k.append(gk[ROWS : ROWS + TILE].astype(jnp.bfloat16))
        border_v.append(gv[ROWS : ROWS + TILE].astype(jnp.bfloat16))
        for span, grad in ((k_span, gk), (v_span, gv)):
            sent = grad[ROWS + TILE :].astype(jnp.bfloat16)
            all_ref[far, span] = sent
            back1_ref[block, :, span] = sent[:TILE]
            back2_ref[block, :, span] = sent[TILE:]
    for block in range(2):
        other = pl.ds(
            pl.multiple_of((1 - block) * ROWS + ids_ref[1 - block, 0] * TILE, TILE), TILE
        )
        own_ref[other, k_span] += border_k[block].astype(jnp.float32)
        own_ref[other, v_span] += border_v[block].astype(jnp.float32)
    all_ref[:PAIR_ROWS, k_span] = own_ref[:, k_span].astype(jnp.bfloat16)
    all_ref[:PAIR_ROWS, v_span] = own_ref[:, v_span].astype(jnp.bfloat16)


def attention(part, mask, ids, q, kv, g, back):
    pair = 2 * HEAD
    steps = PART // pair

    def flat(rows, shift=0):
        return pl.BlockSpec((rows, pair), lambda j: (0, j + shift))

    def whole(*shape):
        return pl.BlockSpec(shape, lambda j: (0,) * len(shape))

    smem = pl.BlockSpec(memory_space=pltpu.SMEM)
    own, here = flat(PAIR_ROWS), flat(PAIR_ROWS, part * steps)
    shapes = [
        ((PAIR_ROWS, 2 * PART), jnp.float32),
        ((ALL_ROWS, 2 * PART), jnp.bfloat16),
    ]
    border = pl.BlockSpec((2, TILE, 2 * PART), lambda j: (0, 0, part))
    return pl.pallas_call(
        attention_kernel,
        grid=(steps,),
        in_specs=[
            smem, smem, here, flat(ALL_ROWS, part * steps),
            flat(ALL_ROWS, part * steps + HALF // pair), here,
        ]
        + [pl.BlockSpec(memory_space=pl.ANY)] * len(back),
        input_output_aliases={6 + index: 4 + index for index in range(len(back))},
        out_specs=[own, own] + [whole(*shape) for shape, _ in shapes] + [border] * 2,
        out_shape=[jax.ShapeDtypeStruct((PAIR_ROWS, PART), jnp.bfloat16)] * 2
        + [jax.ShapeDtypeStruct(*shape) for shape in shapes]
        + [jax.ShapeDtypeStruct((2, TILE, 2 * HALF), jnp.bfloat16)] * 2,
        scratch_shapes=[
            pltpu.VMEM((2 * ROWS, ROWS), jnp.float32),
            pltpu.VMEM((2 * ROWS, ROWS), jnp.float32),
        ],
        compiler_params=pltpu.CompilerParams(vmem_limit_bytes=(56 if back else 40) * 1024 * 1024),
        cost_estimate=pl.CostEstimate(
            flops=8_000_000_000, bytes_accessed=8_000_000, transcendentals=2_500_000
        ),
        name="attention",
    )(mask, ids, q, kv, kv, g, *back)


def spread(value, axes, count):
    copies = jnp.broadcast_to(value[None], (count,) + value.shape)
    return lax.all_to_all(copies, axes, 0, 0, tiled=True)


def norm_kernel(gain_ref, *refs):
    out_ref = refs[-1]
    row = 0
    for ref in refs[:-1]:
        for at in range(0, ref.shape[0], TILE):
            wide = ref[at : at + TILE].astype(jnp.float32)
            square = jnp.mean(wide * wide, axis=1, keepdims=True) + epsilon
            inverse = lax.rsqrt(square)
            inverse = inverse * (1.5 - 0.5 * square * inverse * inverse)
            out_ref[row : row + TILE] = (wide * inverse * gain_ref[...]).astype(jnp.bfloat16)
            row += TILE


def norm_rows(gain, groups):
    rows = sum(group.shape[0] for group in groups)
    return pl.pallas_call(
        norm_kernel,
        out_shape=jax.ShapeDtypeStruct((rows, 1024), jnp.bfloat16),
        compiler_params=pltpu.CompilerParams(vmem_limit_bytes=40 * 1024 * 1024),
        cost_estimate=pl.CostEstimate(flops=6_000_000, bytes_accessed=5_000_000, transcendentals=1280),
        name="norm_rows",
    )(gain.reshape(1, 1024), *groups)


def norm(features, gain):
    wide = features.astype(jnp.float32)
    inverse = lax.rsqrt(jnp.mean(wide * wide, axis=1, keepdims=True) + epsilon)
    return wide, inverse, (wide * inverse * gain).astype(jnp.bfloat16)


def ring(distance):
    return [(z, (z + distance) % 8) for z in range(8)]


def row_block(value, index):
    return lax.dynamic_slice_in_dim(value, (index & 7) * TILE, TILE, 0)


def gather_ring(own, z):
    blocks = [(0, own)]
    up = down = own
    for step in range(1, 4):
        up = lax.ppermute(up, "z", ring(1))
        down = lax.ppermute(down, "z", ring(-1))
        blocks += [(-step, up), (step, down)]
    middle = own.shape[1] // 2
    up = lax.ppermute(up[:, :middle], "z", ring(1))
    down = lax.ppermute(down[:, middle:], "z", ring(-1))
    blocks.append((4, jnp.concatenate([up, down], 1)))
    out = jnp.zeros((1024, own.shape[1]), own.dtype)
    for distance, block in blocks:
        out = lax.dynamic_update_slice_in_dim(out, block, ((z + distance) & 7) * TILE, 0)
    return out


def terms_kernel(core_ref, rows_ref, kv_ref, q_ref, *refs):
    out_ref, out_term = refs[-1], None
    width = out_ref.shape[-1]
    terms = [
        contract_rows(rows_ref[...], kv_ref[...]),
        contract_rows(rows_ref[:PAIR_ROWS], q_ref[...]),
    ]
    if len(refs) > 1:
        *heads_refs, cot_ref, out_ref, out_term = refs
        place = (pl.program_id(0) + 2 * core_ref[0]) & 3
        for index, heads_ref in enumerate(heads_refs):

            @pl.when(place == index)
            def _():
                if index < 2:
                    out_term[...] = contract_rows(heads_ref[...], cot_ref[...])
                else:
                    out_term[...] = contract_rows(
                        heads_ref[:ROWS], cot_ref[ROWS:]
                    ) + contract_rows(heads_ref[ROWS:], cot_ref[:ROWS])

        width = out_ref.shape[-1]
        terms.append(out_term[...])
    terms = jnp.concatenate([term.astype(jnp.bfloat16) for term in terms], 1)
    for block in range(2):
        for piece in range(8):
            row = block * TILE + piece * SLAB
            for which in range(2):
                out_ref[piece // 4, piece % 4, which, block] = terms[
                    row : row + SLAB, which * width : (which + 1) * width
                ]


def weight_terms(core, rows, grad_kv, grad_q, heads=(), cot=None):
    def whole(value):
        return pl.BlockSpec(value.shape, lambda j, c: (0, 0))

    operands = [rows, grad_kv, grad_q]
    width = 3 * PART // 2
    scratch = []
    if heads:
        operands += [*heads, cot]
        width += HALF // 2
        scratch = [pltpu.VMEM((2 * TILE, HALF), jnp.float32)]
    pieces = pl.pallas_call(
        terms_kernel,
        grid_spec=pltpu.PrefetchScalarGridSpec(
            num_scalar_prefetch=1,
            grid=(4,),
            in_specs=[pl.BlockSpec((ALL_ROWS, 2 * TILE), lambda j, c: (0, j))]
            + [whole(value) for value in operands[1:]],
            out_specs=pl.BlockSpec((2, 4, 2, 2, SLAB, width), lambda j, c: (0, 0, 0, j, 0, 0)),
            scratch_shapes=scratch,
        ),
        out_shape=jax.ShapeDtypeStruct((2, 4, 2, 8, SLAB, width), jnp.bfloat16),
        compiler_params=pltpu.CompilerParams(vmem_limit_bytes=(56 if heads else 40) * 1024 * 1024),
        cost_estimate=pl.CostEstimate(
            flops=2_000_000_000, bytes_accessed=8_000_000, transcendentals=0
        ),
        name="weight_terms",
    )(core.astype(jnp.int32).reshape(1), *operands)
    return pieces.reshape(16, 8, SLAB, width)


def row_gradient_kernel(ids_ref, weight_ref, *refs):
    *refs, first_ref, second_ref, mine_ref, theirs_ref = refs
    for block, out_ref in enumerate((mine_ref, theirs_ref)):
        total = None
        for step in range(HALF // PART):
            own_ref, q_ref = refs[2 * step : 2 * step + 2]
            columns = slice(step * 2 * PART, (step + 1) * 2 * PART)
            tiles = []
            for tile in range(TILES):
                row = block * ROWS + tile * TILE
                grad = own_ref[row : row + TILE]
                for slot, back_ref in enumerate((first_ref, second_ref)):
                    back = back_ref[block, :, columns].astype(jnp.float32)
                    grad += jnp.where(ids_ref[block, slot + 1] == tile, back, 0.0)
                tiles.append(grad.astype(jnp.bfloat16))
            tiles = jnp.concatenate(tiles, 0)
            grads = (tiles[:, :PART], tiles[:, PART:], q_ref[block * ROWS : (block + 1) * ROWS])
            for which, grad in enumerate(grads):
                at = which * HALF + step * PART
                part = times_transpose(grad, weight_ref[:, at : at + PART])
                total = part if total is None else total + part
        out_ref[...] = total


def row_gradients(ids, weight, grad_own, grad_q, returned):
    operands = [ids, weight]
    for pair in zip(grad_own, grad_q):
        operands += pair
    operands += returned
    vmem = pl.BlockSpec(memory_space=pltpu.VMEM)
    return pl.pallas_call(
        row_gradient_kernel,
        in_specs=[pl.BlockSpec(memory_space=pltpu.SMEM)] + [vmem] * (len(operands) - 1),
        out_shape=[jax.ShapeDtypeStruct((ROWS, 1024), jnp.float32)] * 2,
        compiler_params=pltpu.CompilerParams(vmem_limit_bytes=40 * 1024 * 1024),
        cost_estimate=pl.CostEstimate(
            flops=2_500_000_000, bytes_accessed=16_000_000, transcendentals=0
        ),
        name="row_gradients",
    )(*operands)


QUERY_COLUMNS = ((1, 128, 384), (0, 896, 1024), (1, 384, 512))
KEY_COLUMNS = ((0, 0, 256), (0, 384, 640))
VALUE_COLUMNS = ((0, 256, 384), (1, 0, 128), (0, 640, 896))
OUT_COLUMNS = ((1, 512, 1024),)


def unpack_kernel(in_ref, *out_refs):
    columns = (QUERY_COLUMNS, KEY_COLUMNS, VALUE_COLUMNS, OUT_COLUMNS)
    for out_ref, spans in zip(out_refs, columns):
        for y in range(4):
            rows = slice(y * SLAB, (y + 1) * SLAB)
            for side in range(2):
                at = side * HALF
                for which, start, stop in spans:
                    value = in_ref[(y * 2 + which) * 2 + side, :, start:stop]
                    out_ref[rows, at : at + stop - start] = value.astype(jnp.float32)
                    at += stop - start


def unpack(gathered):
    return pl.pallas_call(
        unpack_kernel,
        out_shape=[jax.ShapeDtypeStruct((64, 1024), jnp.float32)] * 4,
        name="unpack",
    )(gathered)


def reduce_arrived(arrived):
    return jnp.sum(arrived.astype(jnp.float32), axis=0).astype(jnp.bfloat16)


def local(
    node_features, norm_gain, query_weight, key_weight, value_weight, out_weight,
    cotangent, pair_mask, border_ids,
):
    core, z, xl = (lax.axis_index(axis) for axis in ("core", "z", "xl"))
    routes = (("xh", SWAP), ("y", [(0, 1), (1, 0), (2, 3), (3, 2)]))

    def half_of(value, which, axis=1):
        return lax.dynamic_slice_in_dim(value, which * HALF, HALF, axis)

    def both(value):
        return jnp.concatenate([value, swap_core(value)], 0)

    first = jnp.concatenate(
        [half_of(weight, core) for weight in (key_weight, value_weight, query_weight, out_weight)],
        1,
    )
    other = lax.ppermute(first, "xl", SWAP)
    own = jnp.concatenate([jnp.where(xl == 0, first, other), jnp.where(xl == 0, other, first)], 0)
    own, features, border_ids = lax.optimization_barrier((own, node_features, border_ids))
    border = [
        lax.ppermute(
            lax.dynamic_slice_in_dim(features, border_ids[0, bit + 1] * TILE, TILE, 0),
            axis,
            route,
        )
        for bit, (axis, route) in enumerate(routes)
    ]
    weights = gather_ring(own, z)
    out_half = weights[:, 3 * HALF :]

    plan = both(jnp.concatenate([pair_mask, jnp.broadcast_to(border_ids, (TILES, TILES))], 1))
    mask = plan[:, : 2 * TILES]
    ids = plan[:: TILES, 2 * TILES :]
    normed = norm_rows(
        norm_gain,
        [features, swap_core(features)] + border + [swap_core(tile) for tile in border],
    )
    cotangents = both(cotangent)
    cot_mine, cot_other = half_of(cotangents, core), half_of(cotangents, 1 - core)

    out_mine = half_of(out_half, core, 0)
    out_other = half_of(out_half, 1 - core, 0)
    out_swapped = swap_core(out_other)
    grad_attended = (
        times_transpose(cot_mine, out_mine) + times_transpose(cot_other, out_swapped)
    ).astype(jnp.bfloat16)

    attended, swapped, grad_q, grad_own, parts, back = ([] for _ in range(6))
    kv = dot(normed, weights[:, : 2 * HALF]).astype(jnp.bfloat16)
    q = dot(normed[:PAIR_ROWS], weights[:, 2 * HALF : 3 * HALF]).astype(jnp.bfloat16)
    for step in range(HALF // PART):
        out, gq, own_kv, gkv, *back = attention(step, mask, ids, q, kv, grad_attended, back)
        attended.append(out)
        swapped.append(swap_core(out))
        grad_q.append(gq)
        grad_own.append(own_kv)
        if step == HALF // PART - 1:
            terms = weight_terms(core, normed, gkv, gq, attended + swapped, cot_mine)
            returned = [lax.ppermute(tiles, *to) for tiles, to in zip(back, routes)]
            terms, attended, swapped, grad_q, returned = lax.optimization_barrier(
                (terms, attended, swapped, grad_q, returned)
            )
        else:
            terms = weight_terms(core, normed, gkv, gq)
            terms, grad_attended = lax.optimization_barrier((terms, grad_attended))
        parts.append(reduce_arrived(lax.all_to_all(terms, PLANE, 0, 0, tiled=True)))
    part = jnp.concatenate(parts, -1)
    swapped = [jnp.concatenate([value[ROWS:], value[:ROWS]], 0) for value in swapped]
    update = dot(
        jnp.concatenate(attended + swapped, 1), jnp.concatenate([out_mine, out_other], 0)
    ).astype(jnp.bfloat16)
    update_mine, update_other = update[:ROWS], swap_core(update[ROWS:])
    layer_update = jnp.concatenate(
        [
            jnp.where(core == 0, update_mine, update_other),
            jnp.where(core == 0, update_other, update_mine),
        ],
        1,
    )

    grad_mine, grad_theirs = row_gradients(ids, weights, grad_own, grad_q, returned)
    scaled = (grad_mine + swap_core(grad_theirs)) * norm_gain
    wide, inverse, _ = norm(node_features, norm_gain)
    inner_mean = jnp.mean(scaled * wide, axis=1, keepdims=True)
    node_gradient = (inverse * scaled - wide * inverse**3 * inner_mean).astype(jnp.bfloat16)
    part, layer_update = lax.optimization_barrier((part, layer_update))
    total = reduce_arrived(lax.all_to_all(part, "z", 0, 0, tiled=True))
    weight_gradients = unpack(spread(total, FACE, 16))

    return layer_update, node_gradient, *weight_gradients


def solution(mesh):
    fine = Mesh(mesh.devices.reshape(4, 2, 2, 8, 2), NODES)
    rows = P(NODES, None)
    weight = P(FSDP, None)
    return jax.shard_map(
        local,
        mesh=fine,
        in_specs=(rows, P(), weight, weight, weight, weight, rows, rows, rows),
        out_specs=(rows, rows, weight, weight, weight, weight),
        check_vma=False,
    )
```
